32 devices in a mesh: ctx: 16 (over z, y, core), head: 2 (over x).
Axes of the slice: x: 2, y: 2, z: 4, core: 2. Of those that a mesh axis runs over, the one named last changes fastest.
Arguments:
- queries: bfloat16 [16384, 4096], P('ctx', 'head'), may hold values from -10 to 10, as said below
- keys: bfloat16 [16384, 4096], P('ctx', 'head'), may hold values from -4.6 to 4.6, as said below
- values: bfloat16 [16384, 4096], P('ctx', 'head'), may hold values from -6 to 6
Outputs:
- attended: bfloat16 [16384, 4096], P('ctx', 'head')
The draws below stay inside these ranges and needn't reach their ends.
Inputs may be any that keep to these rules, and one draw needn't show every extreme that they name: real-valued queries. real-valued keys.
All inputs are finite; a program needn't handle non-finite values.
Results may differ from the reference program's by a relative error of at most 0.0099.
Values may be sent and summed in bfloat16 or wider, within the bound.
A program may use at most 128 MiB of HBM per device.

```python
import jax
import jax.numpy as jnp
from jax import lax

HEADS = 32
HD = 128
TOK_DEV = 1024
POOL = 256
EDGE = 256
SEQ = 16384
LEVELS = 4
N_CTX = 16


def draw_queries(key, part):
    noise_key = jax.random.fold_in(key, 1)
    base = jnp.clip(2.5 * jax.random.normal(noise_key, (SEQ, HEADS * HD), jnp.float32), -10.0, 10.0)
    return base.astype(jnp.bfloat16)


def draw_keys(key, part):
    noise_key = jax.random.fold_in(key, 2)
    base = jnp.clip(jax.random.normal(noise_key, (SEQ, HEADS * HD), jnp.float32), -4.0, 4.0)
    return base.astype(jnp.bfloat16)


def level_of(rng, extent, cuts, least, high):
    def one(position, shards_of):
        steps = jax.random.uniform(jax.random.fold_in(jax.random.fold_in(rng, 6), position), (shards_of,), jnp.float32, least / len(cuts), high / len(cuts))
        return jnp.repeat(jnp.exp(steps), extent[position] // shards_of).reshape((-1,) + (1,) * (len(extent) - position - 1))

    loudness = one(*cuts[0])
    for cut in cuts[1:]:
        loudness = loudness * one(*cut)
    return loudness


def noise(rng, dims, scale, bound, shards=(), held_as=jnp.bfloat16):
    values = scale * jax.random.normal(rng, dims, jnp.float32)
    if shards:
        values = values * level_of(rng, dims, shards, -0.22, 0.18)
    return jnp.clip(values, -bound, bound).astype(held_as)


def setup_inputs(seed: int = 0) -> dict:
    streams_of = jax.random.split(jax.random.key(seed), 4)
    queries = draw_queries(jax.random.fold_in(streams_of[3], 71), 0)
    keys = draw_keys(jax.random.fold_in(streams_of[3], 71), 0)
    values = noise(streams_of[2], (SEQ, HEADS * HD), 1.0, 6.0, ((0, 16), (1, 2)))
    return dict(queries=queries, keys=keys, values=values)


def pool_rows(block, group):
    shape = block.shape
    grouped = block.reshape(shape[:-2] + (shape[-2] // group, group, shape[-1])).astype(jnp.float32)
    return (jnp.sum(grouped, axis=-2) / jnp.float32(group ** 0.5)).astype(jnp.bfloat16)


def reference(queries, keys, values):
    width = HEADS * HD
    scale = jnp.float32(HD ** -0.5)
    query_blocks = queries.reshape(N_CTX, TOK_DEV, width)
    paired = jnp.stack((keys.reshape(N_CTX, TOK_DEV, width), values.reshape(N_CTX, TOK_DEV, width)))
    summaries = []
    level = pool_rows(paired, TOK_DEV // POOL)
    for depth in range(LEVELS):
        summaries.append(level)
        if depth + 1 < LEVELS:
            merged = level.reshape(2, N_CTX // (2 ** (depth + 1)), 2 * POOL, width)
            level = pool_rows(merged, 2)
    blank = jnp.zeros((2, 1, TOK_DEV, width), jnp.bfloat16)
    padded = jnp.concatenate([blank, paired, blank], axis=1)

    def one_block(index):
        own = lax.dynamic_index_in_dim(paired, index, 1, keepdims=False)
        left = lax.dynamic_index_in_dim(padded, index, 1, keepdims=False)[:, TOK_DEV - EDGE:]
        right = lax.dynamic_index_in_dim(padded, index + 2, 1, keepdims=False)[:, :EDGE]
        pieces = [own, left, right]
        for depth in range(LEVELS):
            sibling = jnp.bitwise_xor(index // (2 ** depth), 1).astype(jnp.int32)
            pieces.append(lax.dynamic_index_in_dim(summaries[depth], sibling, 1, keepdims=False))
        key_set = jnp.concatenate(pieces, axis=1)
        total = key_set.shape[1]
        valid = jnp.concatenate([
            jnp.ones((TOK_DEV,), bool),
            jnp.broadcast_to(index > 0, (EDGE,)),
            jnp.broadcast_to(index < N_CTX - 1, (EDGE,)),
            jnp.ones((total - TOK_DEV - 2 * EDGE,), bool)])
        query = lax.dynamic_index_in_dim(query_blocks, index, 0, keepdims=False)
        query = query.astype(jnp.float32).reshape(TOK_DEV, HEADS, HD)
        key_all = key_set[0].astype(jnp.float32).reshape(total, HEADS, HD)
        value_all = key_set[1].astype(jnp.float32).reshape(total, HEADS, HD)
        scores = jnp.einsum('qhd,khd->hqk', query, key_all) * scale
        scores = jnp.where(valid[None, None, :], scores, jnp.float32(-1e30))
        peak = jnp.max(scores, axis=-1, keepdims=True)
        probs = jnp.exp(scores - peak)
        denom = jnp.sum(probs, axis=-1)
        weights = probs.astype(jnp.bfloat16)
        numer = jnp.einsum('hqk,khd->qhd', weights.astype(jnp.float32), value_all)
        result = numer / jnp.transpose(denom)[:, :, None]
        return result.astype(jnp.bfloat16).reshape(TOK_DEV, width)

    outputs = lax.map(one_block, jnp.arange(N_CTX, dtype=jnp.int32))
    return outputs.reshape(SEQ, width)
```

```python
import functools
import math

import jax
import jax.numpy as jnp
from jax import lax
from jax.experimental import pallas as pl
from jax.experimental.pallas import tpu as pltpu
from jax.sharding import PartitionSpec as P

HD = 128
POOL = 256
EDGE = 256
SCALE2 = math.log2(math.e) * HD**-0.5
F32 = jnp.float32
BF16 = jnp.bfloat16


def stage_body(kinds, sizes, has_state, final, q_rows, key_cols, *refs):
    flags, q_ref = refs[:2]
    at = 2
    pieces = []
    for _ in kinds:
        pieces.append((refs[at], refs[at + 1]))
        at += 2
    state_ref = None
    if has_state:
        state_ref = refs[at]
        at += 1
    out_ref, k_all, v_all, s_all = refs[at : at + 4]
    total = sum(sizes)
    v_all[:, HD:] = jnp.ones((total, HD), BF16)
    start = 0
    spans = []
    swapped = flags[0] == 1
    for kind, size, (first, second) in zip(kinds, sizes, pieces):
        if kind == "level":
            mine, other = first[...], second[...]
            k_all[start : start + size, :] = jnp.where(swapped, other, mine)
            v_all[start : start + size, :HD] = jnp.where(swapped, mine, other)
        else:
            k_all[start : start + size, :] = first[...]
            v_all[start : start + size, :HD] = second[...]
        flag = {"left": 1, "right": 2}.get(kind)
        step = min(key_cols, size)
        for c in range(start, start + size, step):
            spans.append((c, step, flag))
        start += size
    rows = q_ref.shape[0]
    for r0 in range(0, rows, q_rows):
        q = q_ref[r0 : r0 + q_rows, :]
        slot = (r0 // q_rows) % 2
        peak = None
        for c, width, flag in spans:
            s = lax.dot_general(
                q, k_all[c : c + width, :], (((1,), (1,)), ((), ())), preferred_element_type=F32
            )
            if flag is not None:
                s = jnp.where(flags[flag] == 1, s, F32(-1e30))
            s_all[slot, :, c : c + width] = s
            for j in range(0, width, HD):
                part = s[:, j : j + HD]
                peak = part if peak is None else jnp.maximum(peak, part)
        peak = jnp.max(peak, axis=-1, keepdims=True)
        if has_state:
            before = state_ref[r0 : r0 + q_rows, :]
            old = before[:, 2 * HD - 1 :]
            peak = jnp.maximum(peak, old)
        acc = None
        for c, width, flag in spans:
            p = jnp.exp2((s_all[slot, :, c : c + width] - peak) * F32(SCALE2)).astype(BF16)
            term = jnp.dot(p, v_all[c : c + width, :], preferred_element_type=F32)
            acc = term if acc is None else acc + term
        numer, denom = acc[:, :HD], acc[:, HD:]
        if has_state:
            shrink = jnp.exp2((old - peak) * F32(SCALE2))
            numer = numer + before[:, :HD] * shrink
            denom = denom + before[:, HD : HD + 1] * shrink
        if final:
            out_ref[r0 : r0 + q_rows, :] = (numer / denom).astype(BF16)
        else:
            lane = lax.broadcasted_iota(jnp.int32, (q_rows, HD), 1)
            out_ref[r0 : r0 + q_rows, :HD] = numer
            out_ref[r0 : r0 + q_rows, HD:] = jnp.where(lane < HD // 2, denom, peak)


def stage(flags, queries, pieces, state, final, name, q_rows=128, key_cols=512):
    rows, width = queries.shape
    heads = width // HD
    kinds = [p[0] for p in pieces]
    sizes = [p[1].shape[0] for p in pieces]
    total = sum(sizes)
    specs = [pl.BlockSpec(memory_space=pltpu.SMEM), pl.BlockSpec((rows, HD), lambda h: (0, h))]
    args = [flags, queries]
    for _, first, second in pieces:
        for a in (first, second):
            specs.append(pl.BlockSpec((a.shape[0], HD), lambda h: (0, h)))
            args.append(a)
    if state is not None:
        specs.append(pl.BlockSpec((rows, 2 * HD), lambda h: (0, h)))
        args.append(state)
    out = (
        jax.ShapeDtypeStruct((rows, width), BF16)
        if final
        else jax.ShapeDtypeStruct((rows, 2 * width), F32)
    )
    return pl.pallas_call(
        functools.partial(
            stage_body, kinds, sizes, state is not None, final, min(q_rows, rows), key_cols
        ),
        grid=(heads,),
        in_specs=specs,
        out_specs=pl.BlockSpec((rows, HD if final else 2 * HD), lambda h: (0, h)),
        out_shape=out,
        scratch_shapes=[
            pltpu.VMEM((total, HD), BF16),
            pltpu.VMEM((total, 2 * HD), BF16),
            pltpu.VMEM((2, min(q_rows, rows), total), F32),
        ],
        compiler_params=pltpu.CompilerParams(vmem_limit_bytes=40 * 2**20),
        cost_estimate=pl.CostEstimate(
            flops=rows * total * heads,
            bytes_accessed=rows * HD,
            transcendentals=0,
        ),
        name=name,
    )(*args)


def pooling(out_rows, in_rows, group, offset=0):
    r = lax.broadcasted_iota(jnp.int32, (out_rows, in_rows), 0)
    c = lax.broadcasted_iota(jnp.int32, (out_rows, in_rows), 1)
    return (r - offset == c // group).astype(BF16)


def mm(a, b):
    return jnp.dot(a, b, preferred_element_type=F32)


def on_device(queries, keys, values):
    tok, width = queries.shape
    count = lax.axis_size("ctx")
    depths = count.bit_length() - 1
    pos = lax.axis_index("ctx")
    odd = pos % 2 == 1

    def swap(x, bit):
        return lax.ppermute(x, "ctx", [(i, i ^ 2**bit) for i in range(count)])

    up = [(i, i + 1) for i in range(count - 1)]
    down = [(i + 1, i) for i in range(count - 1)]
    flags = jnp.stack([pos % 2, (pos > 0).astype(jnp.int32), (pos < count - 1).astype(jnp.int32)])
    flags = flags.astype(jnp.int32)

    group = tok // POOL
    m0 = pooling(POOL, tok, group)
    k0 = (mm(m0, keys) / F32(group**0.5)).astype(BF16)
    v0 = (mm(m0, values) / F32(group**0.5)).astype(BF16)
    sib_k0, sib_v0 = swap(k0, 0), swap(v0, 0)
    levels = [("plain", sib_k0, sib_v0)]
    mine = jnp.where(odd, v0, k0)
    partner = jnp.where(odd, sib_v0, sib_k0)
    for depth in range(1, depths):
        upper = pos // 2 ** (depth - 1) % 2
        half = POOL // 2
        own_m = pooling(POOL, POOL, 2, upper * half)
        sib_m = pooling(POOL, POOL, 2, (1 - upper) * half)
        mine = ((mm(own_m, mine) + mm(sib_m, partner)) / F32(2**0.5)).astype(BF16)
        if depth == 1:
            ends = [x for a in (keys, values) for x in (a[tok - EDGE :], a[:EDGE])]
        if depth < 3:
            partner = swap(mine, depth)
        else:
            bit = pos // 2 ** (depth - 1) % 2
            near = swap(lax.dynamic_slice_in_dim(mine, bit * half, half, 0), depth)
            near, state = lax.optimization_barrier(
                (near, stage(flags, queries, [waiting], state, False, "tree"))
            )
            far = swap(near, depth - 1)
            low = jnp.where(bit == 1, far, near)
            high = jnp.where(bit == 1, near, far)
            partner = jnp.concatenate([low, high], axis=0)
        if depth == 1:
            left_k, left_v = lax.ppermute(ends[0], "ctx", up), lax.ppermute(ends[2], "ctx", up)
            right_k, right_v = lax.ppermute(ends[1], "ctx", down), lax.ppermute(ends[3], "ctx", down)
            sides = [("left", left_k, left_v), ("right", right_k, right_v)]
            state = stage(flags, queries, [("plain", keys, values)], None, False, "own")
            partner, state = lax.optimization_barrier((partner, state))
        elif depth == 2:
            state = stage(flags, queries, levels + [waiting], state, False, "near")
            state = stage(flags, queries, sides, state, False, "sides")
            partner, state = lax.optimization_barrier((partner, state))
        waiting = ("level", partner, swap(partner, 0))
    return stage(flags, queries, [waiting], state, True, "root")


def solution(mesh):
    return jax.shard_map(
        on_device,
        mesh=mesh,
        in_specs=(P("ctx", "head"), P("ctx", "head"), P("ctx", "head")),
        out_specs=P("ctx", "head"),
        check_vma=False,
    )
```

```python
import functools
import math

import jax
import jax.numpy as jnp
from jax import lax
from jax.experimental import pallas as pl
from jax.experimental.pallas import tpu as pltpu
from jax.sharding import PartitionSpec as P

HD = 128
POOL = 256
EDGE = 256
SCALE2 = math.log2(math.e) * HD**-0.5
F32 = jnp.float32
BF16 = jnp.bfloat16


def stage_body(kinds, sizes, has_state, final, q_rows, key_cols, *refs):
    flags, q_ref = refs[:2]
    at = 2
    pieces = []
    for _ in kinds:
        pieces.append((refs[at], refs[at + 1]))
        at += 2
    state_ref = None
    if has_state:
        state_ref = refs[at]
        at += 1
    out_ref, k_all, v_all, s_all = refs[at : at + 4]
    total = sum(sizes)
    v_all[:, HD:] = jnp.ones((total, HD), BF16)
    start = 0
    spans = []
    swapped = flags[0] == 1
    for kind, size, (first, second) in zip(kinds, sizes, pieces):
        if kind == "level":
            mine, other = first[...], second[...]
            k_all[start : start + size, :] = jnp.where(swapped, other, mine)
            v_all[start : start + size, :HD] = jnp.where(swapped, mine, other)
        else:
            k_all[start : start + size, :] = first[...]
            v_all[start : start + size, :HD] = second[...]
        flag = {"left": 1, "right": 2}.get(kind)
        step = min(key_cols, size)
        for c in range(start, start + size, step):
            spans.append((c, step, flag))
        start += size
    rows = q_ref.shape[0]
    for r0 in range(0, rows, q_rows):
        q = q_ref[r0 : r0 + q_rows, :]
        slot = (r0 // q_rows) % 2
        peak = None
        for c, width, flag in spans:
            s = lax.dot_general(
                q, k_all[c : c + width, :], (((1,), (1,)), ((), ())), preferred_element_type=F32
            )
            if flag is not None:
                s = jnp.where(flags[flag] == 1, s, F32(-1e30))
            s_all[slot, :, c : c + width] = s
            for j in range(0, width, HD):
                part = s[:, j : j + HD]
                peak = part if peak is None else jnp.maximum(peak, part)
        peak = jnp.broadcast_to(jnp.max(peak, axis=-1, keepdims=True), (q_rows, HD))
        if has_state:
            before = state_ref[r0 : r0 + q_rows, :]
            old = before[:, 2 * HD :]
            peak = jnp.maximum(peak, old)
        acc = None
        for c, width, flag in spans:
            wide = jnp.concatenate([peak] * (width // HD), axis=1)
            p = jnp.exp2((s_all[slot, :, c : c + width] - wide) * F32(SCALE2)).astype(BF16)
            term = jnp.dot(p, v_all[c : c + width, :], preferred_element_type=F32)
            acc = term if acc is None else acc + term
        numer, denom = acc[:, :HD], acc[:, HD:]
        if has_state:
            shrink = jnp.exp2((old - peak) * F32(SCALE2))
            numer = numer + before[:, :HD] * shrink
            denom = denom + before[:, HD : 2 * HD] * shrink
        if final:
            out_ref[r0 : r0 + q_rows, :] = (numer / denom).astype(BF16)
        else:
            out_ref[r0 : r0 + q_rows, :HD] = numer
            out_ref[r0 : r0 + q_rows, HD : 2 * HD] = denom
            out_ref[r0 : r0 + q_rows, 2 * HD :] = peak


def stage(flags, queries, pieces, state, final, name, q_rows=128, key_cols=512):
    rows, width = queries.shape
    heads = width // HD
    kinds = [p[0] for p in pieces]
    sizes = [p[1].shape[0] for p in pieces]
    total = sum(sizes)
    specs = [pl.BlockSpec(memory_space=pltpu.SMEM), pl.BlockSpec((rows, HD), lambda h: (0, h))]
    args = [flags, queries]
    for _, first, second in pieces:
        for a in (first, second):
            specs.append(pl.BlockSpec((a.shape[0], HD), lambda h: (0, h)))
            args.append(a)
    if state is not None:
        specs.append(pl.BlockSpec((rows, 3 * HD), lambda h: (0, h)))
        args.append(state)
    out = (
        jax.ShapeDtypeStruct((rows, width), BF16)
        if final
        else jax.ShapeDtypeStruct((rows, 3 * width), F32)
    )
    return pl.pallas_call(
        functools.partial(
            stage_body, kinds, sizes, state is not None, final, min(q_rows, rows), key_cols
        ),
        grid=(heads,),
        in_specs=specs,
        out_specs=pl.BlockSpec((rows, HD if final else 3 * HD), lambda h: (0, h)),
        out_shape=out,
        scratch_shapes=[
            pltpu.VMEM((total, HD), BF16),
            pltpu.VMEM((total, 2 * HD), BF16),
            pltpu.VMEM((2, min(q_rows, rows), total), F32),
        ],
        compiler_params=pltpu.CompilerParams(vmem_limit_bytes=40 * 2**20),
        cost_estimate=pl.CostEstimate(
            flops=rows * total * heads,
            bytes_accessed=rows * HD,
            transcendentals=0,
        ),
        name=name,
    )(*args)


def pooling(out_rows, in_rows, group, offset=0):
    r = lax.broadcasted_iota(jnp.int32, (out_rows, in_rows), 0)
    c = lax.broadcasted_iota(jnp.int32, (out_rows, in_rows), 1)
    return (r - offset == c // group).astype(BF16)


def mm(a, b):
    return jnp.dot(a, b, preferred_element_type=F32)


def on_device(queries, keys, values):
    tok, width = queries.shape
    count = lax.axis_size("ctx")
    depths = count.bit_length() - 1
    pos = lax.axis_index("ctx")
    odd = pos % 2 == 1

    def swap(x, bit):
        return lax.ppermute(x, "ctx", [(i, i ^ 2**bit) for i in range(count)])

    up = [(i, i + 1) for i in range(count - 1)]
    down = [(i + 1, i) for i in range(count - 1)]
    flags = jnp.stack([pos % 2, (pos > 0).astype(jnp.int32), (pos < count - 1).astype(jnp.int32)])
    flags = flags.astype(jnp.int32)

    group = tok // POOL
    m0 = pooling(POOL, tok, group)
    k0 = (mm(m0, keys) / F32(group**0.5)).astype(BF16)
    v0 = (mm(m0, values) / F32(group**0.5)).astype(BF16)
    sib_k0, sib_v0 = swap(k0, 0), swap(v0, 0)
    levels = [("plain", sib_k0, sib_v0)]
    mine = jnp.where(odd, v0, k0)
    partner = jnp.where(odd, sib_v0, sib_k0)
    for depth in range(1, depths):
        upper = pos // 2 ** (depth - 1) % 2
        half = POOL // 2
        own_m = pooling(POOL, POOL, 2, upper * half)
        sib_m = pooling(POOL, POOL, 2, (1 - upper) * half)
        mine = ((mm(own_m, mine) + mm(sib_m, partner)) / F32(2**0.5)).astype(BF16)
        if depth == 1:
            ends = [x for a in (keys, values) for x in (a[tok - EDGE :], a[:EDGE])]
        if depth < 3:
            partner = swap(mine, depth)
        else:
            bit = pos // 2 ** (depth - 1) % 2
            near = swap(lax.dynamic_slice_in_dim(mine, bit * half, half, 0), depth)
            near, state = lax.optimization_barrier(
                (near, stage(flags, queries, sides + [waiting], state, False, "tree"))
            )
            sides = []
            far = swap(near, depth - 1)
            low = jnp.where(bit == 1, far, near)
            high = jnp.where(bit == 1, near, far)
            partner = jnp.concatenate([low, high], axis=0)
        if depth == 1:
            left_k, left_v = lax.ppermute(ends[0], "ctx", up), lax.ppermute(ends[2], "ctx", up)
            right_k, right_v = lax.ppermute(ends[1], "ctx", down), lax.ppermute(ends[3], "ctx", down)
            sides = [("left", left_k, left_v), ("right", right_k, right_v)]
            state = stage(flags, queries, [("plain", keys, values)], None, False, "own")
            partner, state = lax.optimization_barrier((partner, state))
        elif depth == 2:
            state = stage(flags, queries, levels + [waiting], state, False, "near")
            partner, state = lax.optimization_barrier((partner, state))
        waiting = ("level", partner, swap(partner, 0))
    return stage(flags, queries, [waiting], state, True, "root")


def solution(mesh):
    return jax.shard_map(
        on_device,
        mesh=mesh,
        in_specs=(P("ctx", "head"), P("ctx", "head"), P("ctx", "head")),
        out_specs=P("ctx", "head"),
        check_vma=False,
    )
```
